128 devices in a mesh: ctx: 32 (over x, y_hi, z), fsdp: 4 (over y_lo, core).
Axes of the slice: x: 4, y: 4 (y_hi: 2, y_lo: 2; y = y_hi * 2 + y_lo), z: 4, core: 2. Of those that a mesh axis runs over, the one named last changes fastest.
Arguments:
- query: bfloat16 [4, 8192, 4096], P('fsdp', None, 'ctx'), may hold values from -6 to 6
- gated: bfloat16 [4, 8192, 4096], P('fsdp', None, 'ctx'), may hold values from -6 to 6
- grad_out: bfloat16 [4, 8192, 4096], P('fsdp', None, 'ctx'), may hold values from -6 to 6
- filters: float32 [512, 128], P('fsdp'), may hold values from -0.5 to 0.5
Outputs:
- grad_query: bfloat16 [4, 8192, 4096], P('fsdp', None, 'ctx')
- grad_gated: bfloat16 [4, 8192, 4096], P('fsdp', None, 'ctx')
- grad_filters: float32 [512, 128], P('fsdp')
The draws below stay inside these ranges and needn't reach their ends.
All inputs are finite; a program needn't handle non-finite values.
Results may differ from the reference program's by a relative error of at most 0.0058.
Values may be sent and summed in bfloat16 or wider, within the bound.
No kernel may reach another device: no remote copies, remote signals or barrier semaphores. Data moves between devices by JAX's collectives and lax.ppermute only.
A program may use at most 384 MiB of HBM per device.

```python
import math
import jax
import jax.numpy as jnp
from jax import lax

D = 8192
FLEN = 128
GROUP_CH = 16
GROUPS = 512
TOKENS = 4096
SEQS = 4


def shard_levels(own_key, dims, split, low, high):
    def one(axis_at, parts):
        heights = jax.random.uniform(jax.random.fold_in(jax.random.fold_in(own_key, 6), axis_at), (parts,), jnp.float32, low / len(split), high / len(split))
        return jnp.repeat(jnp.exp(heights), dims[axis_at] // parts).reshape((-1,) + (1,) * (len(dims) - axis_at - 1))

    gain = one(*split[0])
    for cut in split[1:]:
        gain = gain * one(*cut)
    return gain


def centred(own_key, dims, deviation, bound, pieces=(), held_as=jnp.bfloat16):
    entries = deviation * jax.random.normal(own_key, dims, jnp.float32)
    if pieces:
        entries = entries * shard_levels(own_key, dims, pieces, -0.22, 0.18)
    return jnp.clip(entries, -bound, bound).astype(held_as)


def setup_inputs(seed: int = 0) -> dict:
    splits = jax.random.split(jax.random.key(seed), 5)
    query = centred(splits[0], (SEQS, D, TOKENS), 1.0, 6.0, ((0, 4), (2, 32)))
    gated = centred(splits[1], (SEQS, D, TOKENS), 1.0, 6.0, ((0, 4), (2, 32)))
    grad_out = centred(splits[2], (SEQS, D, TOKENS), 1.0, 6.0, ((0, 4), (2, 32)))
    filters = centred(splits[3], (GROUPS, FLEN), FLEN ** -0.5, 0.5, ((0, 4),), jnp.float32)
    return {"query": query, "gated": gated, "grad_out": grad_out, "filters": filters}


def build_band(taps):
    groups, length = taps.shape
    row = jnp.concatenate([taps[:, ::-1], jnp.zeros((groups, length + 1), taps.dtype)], axis=1)
    flat = jnp.tile(row, (1, length))
    flat = jnp.concatenate([jnp.zeros((groups, 1), taps.dtype), flat], axis=1)[:, :length * 2 * length]
    return flat.reshape(groups, length, 2 * length)

def fold_taps(outer):
    groups, length = (outer.shape[0], outer.shape[1])
    flat = outer.reshape(groups, length * 2 * length)
    flat = jnp.concatenate([flat, jnp.zeros((groups, length + 1), outer.dtype)], axis=1)
    skewed = flat[:, 1:1 + length * (2 * length + 1)].reshape(groups, length, 2 * length + 1)[:, :, :length]
    return lax.optimization_barrier(jnp.sum(skewed, axis=1))[:, ::-1]

def reference(query, gated, grad_out, filters):
    taps = lax.optimization_barrier(filters.astype(jnp.bfloat16)).astype(jnp.float32)
    band = build_band(taps)
    nblocks = TOKENS // FLEN
    groups = D // GROUP_CH
    tap_sums = jnp.zeros((groups, FLEN), jnp.float32)
    grads_q = []
    grads_z = []
    for seq in range(SEQS):
        blocks = gated[seq].astype(jnp.float32).reshape(D, nblocks, FLEN)
        padded = jnp.concatenate([jnp.zeros((D, 1, FLEN), jnp.float32), blocks], axis=1)
        windows = jnp.concatenate([padded[:, :-1], padded[:, 1:]], axis=2).reshape(groups, GROUP_CH, nblocks, 2 * FLEN)
        conv = jnp.einsum('gim,gcnm->gcni', band, windows).reshape(D, TOKENS)
        cotan = grad_out[seq].astype(jnp.float32)
        grads_q.append((cotan * conv).astype(jnp.bfloat16))
        grad_core = (cotan * query[seq].astype(jnp.float32)).astype(jnp.bfloat16)
        core = lax.optimization_barrier(grad_core).astype(jnp.float32)
        core_blocks = core.reshape(groups, GROUP_CH, nblocks, FLEN)
        spread = jnp.einsum('gim,gcni->gcnm', band, core_blocks)
        later = jnp.concatenate([spread[:, :, 1:, :FLEN], jnp.zeros((groups, GROUP_CH, 1, FLEN), jnp.float32)], axis=2)
        grads_z.append((spread[:, :, :, FLEN:] + later).reshape(D, TOKENS).astype(jnp.bfloat16))
        outer = jnp.einsum('gcni,gcnm->gim', core_blocks, windows)
        tap_sums = tap_sums + fold_taps(outer)
    scale = 1.0 / math.sqrt(SEQS * TOKENS * GROUP_CH)
    return (jnp.stack(grads_q), jnp.stack(grads_z), tap_sums * scale)
```

```python
import math

import jax
import jax.numpy as jnp
import ml_dtypes
import numpy as np
from jax import lax
from jax.experimental import pallas as pl
from jax.experimental.pallas import tpu as pltpu
from jax.sharding import PartitionSpec as P

FLEN = 128
GROUP_CH = 16
WIN = 2 * FLEN
BLOCK = 512
F32, BF16 = jnp.float32, jnp.bfloat16


def split(a):
    hi = a.astype(ml_dtypes.bfloat16)
    lo = (a - hi.astype(np.float64)).astype(ml_dtypes.bfloat16)
    return hi, lo


def tables():
    n = np.arange(WIN)[:, None]
    k = np.arange(FLEN)[None, :]
    angle = np.pi * (((2 * k + 1) * n) % (2 * WIN)) / WIN
    fwd = np.concatenate([np.cos(angle), -np.sin(angle)], axis=1)
    inv = fwd.T / FLEN
    fwd_hi, fwd_lo = split(fwd)
    inv_hi, inv_lo = split(inv)
    fwd2 = np.concatenate([fwd_hi, fwd_lo], axis=0)
    left = np.concatenate([fwd_hi[:FLEN], fwd_lo[:FLEN]], axis=0)
    right = np.concatenate([fwd_hi[FLEN:], fwd_lo[FLEN:]], axis=0)
    inv3 = np.concatenate([inv_hi, inv_hi, inv_lo], axis=0)
    return fwd2, left, right, inv3[:, :FLEN], inv3[:, FLEN:]


def dot(a, b):
    return jnp.dot(a, b, preferred_element_type=F32)


def spectrum(first, second, table):
    return dot(jnp.concatenate([first, second, first, second], axis=1), table)


def half_spectrum(block, table):
    return dot(jnp.concatenate([block, block], axis=1), table)


def invert(re, im, table):
    y = jnp.concatenate([re, im], axis=1)
    hi = y.astype(BF16)
    lo = (y - hi.astype(F32)).astype(BF16)
    return dot(jnp.concatenate([hi, lo, hi], axis=1), table)


def per_channel(h):
    groups = h.shape[0]
    return jnp.broadcast_to(h[:, None, :], (groups, GROUP_CH, FLEN)).reshape(groups * GROUP_CH, FLEN)


def group_sum(x):
    return jnp.sum(x.reshape(x.shape[0] // GROUP_CH, GROUP_CH, FLEN), axis=1)


def convolve(x, h, table):
    hr, hi = per_channel(h[:, :FLEN]), per_channel(h[:, FLEN:])
    xr, xi = x[:, :FLEN], x[:, FLEN:]
    return invert(xr * hr - xi * hi, xr * hi + xi * hr, table)


def correlate(v, h, table):
    hr, hi = per_channel(h[:, :FLEN]), per_channel(h[:, FLEN:])
    vr, vi = v[:, :FLEN], v[:, FLEN:]
    return invert(vr * hr + vi * hi, vi * hr - vr * hi, table)


def cross(a, b):
    ar, ai, br, bi = a[:, :FLEN], a[:, FLEN:], b[:, :FLEN], b[:, FLEN:]
    return jnp.concatenate([group_sum(ar * br + ai * bi), group_sum(ai * br - ar * bi)], axis=1)


def keep(flag, block):
    return jnp.where(flag > 0, block, jnp.zeros_like(block))


def forward(flags, prev, cur, gate, h, fwd2, inv_b, gq):
    x = spectrum(keep(flags[0], prev[...]), cur[...], fwd2[...])
    conv = convolve(x, h[...], inv_b[...])
    gq[...] = (gate[...].astype(F32) * conv).astype(BF16)
    return x


def backward(flags, nxt, core, h, fwd2, inv_a, gg):
    v = spectrum(core[...], keep(flags[1], nxt[...]), fwd2[...])
    gg[...] = correlate(v, h[...], inv_a[...]).astype(BF16)
    return v


def first_kernel(flags, prev, cur_a, gate, core_a, h_a, nxt, core_b, cur_b, h_b, fwd2, left, right, inv_a, inv_b,
                 *rest):
    gq, gg, sums_a, sums_b = rest[-4:]
    x = forward(flags, prev, cur_a, gate, h_a, fwd2, inv_b, gq)
    sums_a[...] = cross(half_spectrum(core_a[...], right[...]), x)
    v = backward(flags, nxt, core_b, h_b, fwd2, inv_a, gg)
    sums_b[...] = cross(v, half_spectrum(cur_b[...], left[...]))


def second_kernel(flags, prev, cur_b, gate, h_b, nxt, core_a, h_a, fwd2, inv_a, inv_b, *rest):
    gq, gg = rest[-2:]
    forward(flags, prev, cur_b, gate, h_b, fwd2, inv_b, gq)
    backward(flags, nxt, core_a, h_a, fwd2, inv_a, gg)


def rows_at(start, width, block):
    return pl.BlockSpec((block, width), lambda i, *_: (start // block + i, 0))


def whole(a):
    return pl.BlockSpec(a.shape, lambda i, *_: (0, 0))


ANY = pl.BlockSpec(memory_space=pl.ANY)


def run(kernel, flags, blocks, consts, carried, outs, count, extra, name):
    width = blocks[0][0].shape[1]
    args = [a for a, _ in blocks] + list(consts)
    specs = [s for _, s in blocks] + [whole(c) for c in consts]
    aliases = {}
    if carried is not None:
        aliases = {1 + len(args): 0, 2 + len(args): 1}
        args += list(carried)
        specs += [ANY, ANY]
    full = jax.ShapeDtypeStruct(outs[0], BF16)
    return pl.pallas_call(
        kernel,
        out_shape=[full, full] + [s for s, _ in extra],
        grid_spec=pltpu.PrefetchScalarGridSpec(
            num_scalar_prefetch=1,
            grid=(count,),
            in_specs=specs,
            out_specs=list(outs[1:]) + [s for _, s in extra],
        ),
        input_output_aliases=aliases,
        compiler_params=pltpu.CompilerParams(vmem_limit_bytes=40 * 1024 * 1024),
        name=name,
    )(flags, *args)


def exchange(x, partner):
    n_ctx, n_fsdp = lax.axis_size("ctx"), lax.axis_size("fsdp")
    pairs = []
    for c in range(n_ctx):
        for f in range(n_fsdp):
            pc, pf = partner(c, f)
            pairs.append((c * n_fsdp + f, pc * n_fsdp + pf))
    return lax.ppermute(x, ("ctx", "fsdp"), pairs)


def reduce_taps(partial):
    f = lax.axis_index("fsdp")
    core, low = f % 2, f // 2
    x = partial.reshape(2, 2, -1, FLEN)
    pick = lambda a, i, axis: lax.dynamic_index_in_dim(a, i, axis, keepdims=False)
    x = pick(x, core, 1) + exchange(pick(x, 1 - core, 1), lambda c, f: (c, f ^ 1))
    x = pick(x, low, 0) + exchange(pick(x, 1 - low, 0), lambda c, f: (c, f ^ 2))
    for partner in (
        lambda c, f: (c ^ 1, f),
        lambda c, f: (c - c % 4 + 3 - c % 4, f),
        lambda c, f: (c ^ 4, f),
        lambda c, f: (c ^ 8, f),
        lambda c, f: ((3 - c // 8) * 8 + c % 8, f),
    ):
        x = x + exchange(x, partner)
    return x


def per_device(query, gated, grad_out, filters):
    query, gated, grad_out = query[0], gated[0], grad_out[0]
    width = gated.shape[0]
    half, quarter = width // 2, width // 4
    n_ctx = lax.axis_size("ctx")
    me = lax.axis_index("ctx")
    flags = jnp.stack([(me > 0), (me < n_ctx - 1)]).astype(jnp.int32)
    fwd2, left, right, inv_a, inv_b = (jnp.asarray(t) for t in tables())
    up = [(i, (i + 1) % n_ctx) for i in range(n_ctx)]
    down = [(b, a) for a, b in up]

    starts = [0, quarter, half, half + quarter]
    part = lambda a, i: lax.slice_in_dim(a, starts[i], starts[i] + quarter, axis=0)
    core = [(part(grad_out, i).astype(F32) * part(query, i).astype(F32)).astype(BF16) for i in range(4)]
    prev = [lax.ppermute(part(gated, i), "ctx", up) for i in (0, 1, 2, 3)]
    nxt = [None] * 4
    for i in (2, 3, 0, 1):
        nxt[i] = lax.ppermute(core[i], "ctx", down)

    taps = lax.all_gather(filters.astype(BF16), "fsdp", axis=0, tiled=True)
    h = dot(jnp.concatenate([taps, taps], axis=1), left)

    steps = quarter // BLOCK
    gb = BLOCK // GROUP_CH
    at = lambda i: rows_at(starts[i], FLEN, BLOCK)
    zero = rows_at(0, FLEN, BLOCK)
    h_at = lambda i: rows_at(starts[i] // GROUP_CH, WIN, gb)
    sums = (jax.ShapeDtypeStruct((quarter // GROUP_CH, WIN), F32), rows_at(0, WIN, gb))

    carried = None
    tap_spec = [None] * 4
    for i, j in ((0, 2), (1, 3)):
        gq, gg, tap_spec[i], tap_spec[j] = run(
            first_kernel,
            flags,
            [(prev[i], zero), (gated, at(i)), (grad_out, at(i)), (core[i], zero), (h, h_at(i)),
             (nxt[j], zero), (core[j], zero), (gated, at(j)), (h, h_at(j))],
            (fwd2, left, right, inv_a, inv_b),
            carried,
            (gated.shape, at(i), at(j)),
            steps,
            [sums, sums],
            "conv_and_taps",
        )
        carried = (gq, gg)
    spec = jnp.concatenate(tap_spec, axis=0)
    partial = invert(spec[:, :FLEN], spec[:, FLEN:], inv_a)
    summed = reduce_taps(partial)
    count = lax.axis_size("fsdp") * n_ctx * FLEN * GROUP_CH
    grad_filters = summed * (1.0 / math.sqrt(count))
    for i, j in ((2, 0), (3, 1)):
        carried = run(
            second_kernel,
            flags,
            [(prev[i], zero), (gated, at(i)), (grad_out, at(i)), (h, h_at(i)),
             (nxt[j], zero), (core[j], zero), (h, h_at(j))],
            (fwd2, inv_a, inv_b),
            carried,
            (gated.shape, at(i), at(j)),
            steps,
            [],
            "conv_only",
        )
    gq, gg = carried
    return (gq[None], gg[None], grad_filters)


def solution(mesh):
    return jax.shard_map(
        per_device,
        mesh=mesh,
        in_specs=(
            P("fsdp", None, "ctx"),
            P("fsdp", None, "ctx"),
            P("fsdp", None, "ctx"),
            P("fsdp", None),
        ),
        out_specs=(P("fsdp", None, "ctx"), P("fsdp", None, "ctx"), P("fsdp", None)),
        check_vma=False,
    )
```

```python
import math

import jax
import jax.numpy as jnp
import ml_dtypes
import numpy as np
from jax import lax
from jax.experimental import pallas as pl
from jax.experimental.pallas import tpu as pltpu
from jax.sharding import PartitionSpec as P

FLEN = 128
GROUP_CH = 16
WIN = 2 * FLEN
BLOCK = 1024
VMEM_MB = 60
F32, BF16 = jnp.float32, jnp.bfloat16


def split(a):
    hi = a.astype(ml_dtypes.bfloat16)
    lo = (a - hi.astype(np.float64)).astype(ml_dtypes.bfloat16)
    return hi, lo


def tables():
    n = np.arange(WIN)[:, None]
    k = np.arange(FLEN)[None, :]
    angle = np.pi * (((2 * k + 1) * n) % (2 * WIN)) / WIN
    fwd = np.concatenate([np.cos(angle), -np.sin(angle)], axis=1)
    inv = fwd.T / FLEN
    fwd_hi, fwd_lo = split(fwd)
    inv_hi, inv_lo = split(inv)
    fwd2 = np.concatenate([fwd_hi, fwd_lo], axis=0)
    left = np.concatenate([fwd_hi[:FLEN], fwd_lo[:FLEN]], axis=0)
    right = np.concatenate([fwd_hi[FLEN:], fwd_lo[FLEN:]], axis=0)
    pair = lambda cols: np.concatenate([inv_hi[:, cols], inv_lo[:, cols]], axis=1)
    return fwd2, left, right, pair(slice(0, FLEN)), pair(slice(FLEN, WIN))


def dot(a, b):
    return jnp.dot(a, b, preferred_element_type=F32)


def spectrum(first, second, table):
    return dot(jnp.concatenate([first, second, first, second], axis=1), table)


def half_spectrum(block, table):
    return dot(jnp.concatenate([block, block], axis=1), table)


def invert(re, im, table):
    y = dot(jnp.concatenate([re.astype(BF16), im.astype(BF16)], axis=1), table)
    return y[:, :FLEN] + y[:, FLEN:]


def invert_wide(y, table):
    hi = y.astype(BF16)
    lo = (y - hi.astype(F32)).astype(BF16)
    a, b = dot(hi, table), dot(lo, table)
    return a[:, :FLEN] + (a[:, FLEN:] + b[:, :FLEN])


def per_channel(h):
    groups = h.shape[0]
    return jnp.broadcast_to(h[:, None, :], (groups, GROUP_CH, FLEN)).reshape(groups * GROUP_CH, FLEN)


def group_sum(x):
    return jnp.sum(x.reshape(x.shape[0] // GROUP_CH, GROUP_CH, FLEN), axis=1)


def convolve(x, h, table):
    hr, hi = per_channel(h[:, :FLEN]), per_channel(h[:, FLEN:])
    xr, xi = x[:, :FLEN], x[:, FLEN:]
    return invert(xr * hr - xi * hi, xr * hi + xi * hr, table)


def correlate(v, h, table):
    hr, hi = per_channel(h[:, :FLEN]), per_channel(h[:, FLEN:])
    vr, vi = v[:, :FLEN], v[:, FLEN:]
    return invert(vr * hr + vi * hi, vi * hr - vr * hi, table)


def cross(a, b):
    ar, ai, br, bi = a[:, :FLEN], a[:, FLEN:], b[:, :FLEN], b[:, FLEN:]
    return jnp.concatenate([group_sum(ar * br + ai * bi), group_sum(ai * br - ar * bi)], axis=1)


def masked(flag, block):
    return jnp.where(flag[...] > 0, block, jnp.zeros_like(block))


def conv_kernel(flag, prev, cur, gate, h, fwd2, inv_b, gq):
    x = spectrum(masked(flag, prev[...]), cur[...], fwd2[...])
    gq[...] = (gate[...].astype(F32) * convolve(x, h[...], inv_b[...])).astype(BF16)
    return x


def corr_kernel(flag, nxt, core, h, fwd2, inv_a, gg):
    v = spectrum(core[...], masked(flag, nxt[...]), fwd2[...])
    gg[...] = correlate(v, h[...], inv_a[...]).astype(BF16)
    return v


def conv_taps_kernel(flag, prev, cur, gate, h, core, fwd2, inv_b, right, inv_a, gq, taps):
    x = conv_kernel(flag, prev, cur, gate, h, fwd2, inv_b, gq)
    taps[...] = invert_wide(cross(half_spectrum(core[...], right[...]), x), inv_a[...])


def corr_taps_kernel(flag, nxt, core, h, cur, fwd2, inv_a, left, gg, taps):
    v = corr_kernel(flag, nxt, core, h, fwd2, inv_a, gg)
    taps[...] = invert_wide(cross(v, half_spectrum(cur[...], left[...])), inv_a[...])


def rows_at(start, width, block):
    return pl.BlockSpec((block, width), lambda i, *_: (start // block + i, 0))


def whole(a):
    return pl.BlockSpec(a.shape, lambda i, *_: (0, 0))


ANY = pl.BlockSpec(memory_space=pl.ANY)


def run(kernel, flag, blocks, consts, out, start, size, carried=None, taps=False, cost=0):
    args = [flag] + [a for a, _ in blocks] + list(consts)
    specs = [whole(flag)] + [s for _, s in blocks] + [whole(c) for c in consts]
    drop, aliases = None, {}
    if carried is not None:
        at = len(args)
        aliases = {at: 0}
        args.append(carried)
        specs.append(ANY)
        drop = at
    shapes = [jax.ShapeDtypeStruct(out.shape, BF16)]
    outs = [rows_at(start, FLEN, BLOCK)]
    if taps:
        shapes.append(jax.ShapeDtypeStruct((size // GROUP_CH, FLEN), F32))
        outs.append(rows_at(0, FLEN, BLOCK // GROUP_CH))

    def body(*refs):
        kernel(*(r for i, r in enumerate(refs) if i != drop))

    return pl.pallas_call(
        body,
        out_shape=shapes,
        grid=(size // BLOCK,),
        in_specs=specs,
        out_specs=outs,
        input_output_aliases=aliases,
        compiler_params=pltpu.CompilerParams(vmem_limit_bytes=VMEM_MB * 1024 * 1024),
        cost_estimate=pl.CostEstimate(flops=cost * 10**9, bytes_accessed=cost * 10**7, transcendentals=0),
        name=kernel.__name__,
    )(*args)


def exchange(x, partner):
    n_ctx, n_fsdp = lax.axis_size("ctx"), lax.axis_size("fsdp")
    pairs = []
    for c in range(n_ctx):
        for f in range(n_fsdp):
            to = partner(c, f)
            if to is not None:
                pairs.append((c * n_fsdp + f, to[0] * n_fsdp + to[1]))
    return lax.ppermute(x, ("ctx", "fsdp"), pairs)


def after(array, done):
    return lax.optimization_barrier((array, done))[0]


def pick(a, i, axis):
    return lax.dynamic_index_in_dim(a, i, axis, keepdims=False)


def reduce_taps(x):
    core, low = lax.axis_index("fsdp") % 2, lax.axis_index("fsdp") // 2
    x = pick(x, core, 1) + exchange(pick(x, 1 - core, 1), lambda c, f: (c, f ^ 1))
    x = pick(x, low, 0) + exchange(pick(x, 1 - low, 0), lambda c, f: (c, f ^ 2))
    for partner in (
        lambda c, f: (c ^ 8, f),
        lambda c, f: ((3 - c // 8) * 8 + c % 8, f),
        lambda c, f: (c ^ 4, f),
        lambda c, f: (c ^ 1, f),
        lambda c, f: (c // 4 * 4 + 3 - c % 4, f),
    ):
        x = x + exchange(x, partner)
    return x


def per_device(query, gated, grad_out, filters):
    query, gated, grad_out = query[0], gated[0], grad_out[0]
    width = gated.shape[0]
    half = width // 2
    n_ctx = lax.axis_size("ctx")
    me = lax.axis_index("ctx")
    has_prev = jnp.full((1, FLEN), me > 0, BF16)
    has_next = jnp.full((1, FLEN), me < n_ctx - 1, BF16)
    fwd2, left, right, inv_a, inv_b = (jnp.asarray(t) for t in tables())
    up = [(i, (i + 1) % n_ctx) for i in range(n_ctx)]
    down = [(b, a) for a, b in up]

    rows = lambda a, start, size: lax.slice_in_dim(a, start, start + size, axis=0)
    product = lambda o, q, start, size: (rows(o, start, size).astype(F32) * rows(q, start, size).astype(F32)).astype(BF16)
    h_at = lambda start: rows_at(start // GROUP_CH, WIN, BLOCK // GROUP_CH)
    at = lambda start: rows_at(start, FLEN, BLOCK)

    fsdp = lax.axis_index("fsdp")
    far = exchange(filters, lambda c, f: (c, f ^ 2))
    column = jnp.where(fsdp // 2 == 0, jnp.stack([filters, far]), jnp.stack([far, filters])).astype(BF16)
    near = exchange(column, lambda c, f: (c, f ^ 1))
    taps = jnp.where(fsdp % 2 == 0, jnp.stack([column, near], axis=1), jnp.stack([near, column], axis=1)).reshape(-1, FLEN)
    h = dot(jnp.concatenate([taps, taps], axis=1), left)

    core_b = product(grad_out, query, half, half)
    sent_a, core_b, _ = lax.optimization_barrier((rows(gated, 0, half), core_b, far))
    prev_a = lax.ppermute(sent_a, "ctx", up)
    nxt_b = lax.ppermute(core_b, "ctx", down)
    late = lax.optimization_barrier((gated, grad_out, query, core_b))[:3]
    core_a = product(late[1], late[2], 0, half)
    prev_b = lax.ppermute(rows(late[0], half, half), "ctx", up)
    nxt_a = lax.ppermute(core_a, "ctx", down)

    gq, taps_a = run(
        conv_taps_kernel,
        has_prev,
        [(prev_a, at(0)), (gated, at(0)), (grad_out, at(0)), (h, h_at(0)), (core_a, at(0))],
        (fwd2, inv_b, right, inv_a),
        gated, 0, half, taps=True,
    )
    has_next, _ = lax.optimization_barrier((has_next, taps_a))
    gg, taps_b = run(
        corr_taps_kernel,
        has_next,
        [(nxt_b, at(0)), (core_b, at(0)), (h, h_at(half)), (gated, at(half))],
        (fwd2, inv_a, left),
        gated, half, half, taps=True,
    )
    partial = jnp.stack([taps_a, taps_b]).reshape(2, 2, -1, FLEN)
    prev_b, nxt_a, partial = lax.optimization_barrier((prev_b, nxt_a, partial))
    summed = reduce_taps(partial)
    gq, = run(
        conv_kernel,
        has_prev,
        [(prev_b, at(0)), (gated, at(half)), (grad_out, at(half)), (h, h_at(half))],
        (fwd2, inv_b),
        gated, half, half, carried=gq, cost=1,
    )
    gg, = run(
        corr_kernel,
        has_next,
        [(nxt_a, at(0)), (core_a, at(0)), (h, h_at(0))],
        (fwd2, inv_a),
        gated, 0, half, carried=gg, cost=1,
    )
    count = lax.axis_size("fsdp") * n_ctx * FLEN * GROUP_CH
    grad_filters = summed * (1.0 / math.sqrt(count))
    return (gq[None], gg[None], grad_filters)


def solution(mesh):
    return jax.shard_map(
        per_device,
        mesh=mesh,
        in_specs=(
            P("fsdp", None, "ctx"),
            P("fsdp", None, "ctx"),
            P("fsdp", None, "ctx"),
            P("fsdp", None),
        ),
        out_specs=(P("fsdp", None, "ctx"), P("fsdp", None, "ctx"), P("fsdp", None)),
        check_vma=False,
    )
```

```python
import math

import jax
import jax.numpy as jnp
import ml_dtypes
import numpy as np
from jax import lax
from jax.experimental import pallas as pl
from jax.experimental.pallas import tpu as pltpu
from jax.sharding import PartitionSpec as P

FLEN = 128
GROUP_CH = 16
WIN = 2 * FLEN
BLOCK = 1024
VMEM_MB = 63
F32, BF16 = jnp.float32, jnp.bfloat16


def split(a):
    hi = a.astype(ml_dtypes.bfloat16)
    lo = (a - hi.astype(np.float64)).astype(ml_dtypes.bfloat16)
    return hi, lo


def tables():
    n = np.arange(WIN)[:, None]
    k = np.arange(FLEN)[None, :]
    angle = np.pi * (((2 * k + 1) * n) % (2 * WIN)) / WIN
    fwd = np.concatenate([np.cos(angle), -np.sin(angle)], axis=1)
    inv = fwd.T / FLEN
    fwd_hi, fwd_lo = split(fwd)
    inv_hi, inv_lo = split(inv)
    fwd2 = np.concatenate([fwd_hi, fwd_lo], axis=0)
    left = np.concatenate([fwd_hi[:FLEN], fwd_lo[:FLEN]], axis=0)
    right = np.concatenate([fwd_hi[FLEN:], fwd_lo[FLEN:]], axis=0)
    pair = lambda cols: np.concatenate([inv_hi[:, cols], inv_lo[:, cols]], axis=1)
    return fwd2, left, right, pair(slice(0, FLEN)), pair(slice(FLEN, WIN))


def dot(a, b):
    return jnp.dot(a, b, preferred_element_type=F32)


def spectrum(first, second, table):
    return dot(jnp.concatenate([first, second, first, second], axis=1), table)


def half_spectrum(block, table):
    return dot(jnp.concatenate([block, block], axis=1), table)


def invert(re, im, table):
    y = dot(jnp.concatenate([re.astype(BF16), im.astype(BF16)], axis=1), table)
    return y[:, :FLEN] + y[:, FLEN:]


def invert_wide(y, table):
    hi = y.astype(BF16)
    lo = (y - hi.astype(F32)).astype(BF16)
    a, b = dot(hi, table), dot(lo, table)
    return a[:, :FLEN] + (a[:, FLEN:] + b[:, :FLEN])


def per_channel(h):
    groups = h.shape[0]
    return jnp.broadcast_to(h[:, None, :], (groups, GROUP_CH, FLEN)).reshape(groups * GROUP_CH, FLEN)


def group_sum(x):
    return jnp.sum(x.reshape(x.shape[0] // GROUP_CH, GROUP_CH, FLEN), axis=1)


def convolve(x, h, table):
    hr, hi = per_channel(h[:, :FLEN]), per_channel(h[:, FLEN:])
    xr, xi = x[:, :FLEN], x[:, FLEN:]
    return invert(xr * hr - xi * hi, xr * hi + xi * hr, table)


def correlate(v, h, table):
    hr, hi = per_channel(h[:, :FLEN]), per_channel(h[:, FLEN:])
    vr, vi = v[:, :FLEN], v[:, FLEN:]
    return invert(vr * hr + vi * hi, vi * hr - vr * hi, table)


def cross(a, b):
    ar, ai, br, bi = a[:, :FLEN], a[:, FLEN:], b[:, :FLEN], b[:, FLEN:]
    return jnp.concatenate([group_sum(ar * br + ai * bi), group_sum(ai * br - ar * bi)], axis=1)


def masked(present, block):
    return jnp.where(present, block, jnp.zeros_like(block))


def has_previous():
    return lax.axis_index("ctx") > 0


def has_next():
    return lax.axis_index("ctx") < lax.axis_size("ctx") - 1


def conv_kernel(prev, cur, gate, h, fwd2, inv_b, gq):
    x = spectrum(masked(has_previous(), prev[...]), cur[...], fwd2[...])
    gq[...] = (gate[...].astype(F32) * convolve(x, h[...], inv_b[...])).astype(BF16)
    return x


def corr_kernel(nxt, core, h, fwd2, inv_a, gg):
    v = spectrum(core[...], masked(has_next(), nxt[...]), fwd2[...])
    gg[...] = correlate(v, h[...], inv_a[...]).astype(BF16)
    return v


def conv_taps_kernel(prev, cur, gate, h, core, fwd2, inv_b, right, inv_a, gq, taps):
    x = conv_kernel(prev, cur, gate, h, fwd2, inv_b, gq)
    taps[...] = invert_wide(cross(half_spectrum(core[...], right[...]), x), inv_a[...])


def corr_taps_kernel(nxt, core, h, cur, fwd2, inv_a, left, gg, taps):
    v = corr_kernel(nxt, core, h, fwd2, inv_a, gg)
    taps[...] = invert_wide(cross(v, half_spectrum(cur[...], left[...])), inv_a[...])


def rows_at(start, width, block):
    return pl.BlockSpec((block, width), lambda i, *_: (start // block + i, 0))


def whole(a):
    return pl.BlockSpec(a.shape, lambda i, *_: (0, 0))


ANY = pl.BlockSpec(memory_space=pl.ANY)


def run(kernel, blocks, consts, results, size, cost=0):
    args = [a for a, _ in blocks] + list(consts)
    specs = [s for _, s in blocks] + [whole(c) for c in consts]
    used, aliases = len(args), {}
    for i, (out, _, _) in enumerate(results):
        if not isinstance(out, jax.ShapeDtypeStruct):
            aliases[len(args)] = i
            args.append(out)
            specs.append(ANY)
    given = len(args)

    def body(*refs):
        kernel(*refs[:used], *refs[given:])

    return pl.pallas_call(
        body,
        out_shape=[jax.ShapeDtypeStruct(out.shape, out.dtype) for out, _, _ in results],
        grid=(size // BLOCK,),
        in_specs=specs,
        out_specs=[rows_at(start, FLEN, block) for _, start, block in results],
        input_output_aliases=aliases,
        compiler_params=pltpu.CompilerParams(vmem_limit_bytes=VMEM_MB * 1024 * 1024),
        cost_estimate=pl.CostEstimate(flops=cost * 10**9, bytes_accessed=cost * 10**7, transcendentals=0),
        name=kernel.__name__,
    )(*args)


def exchange(x, partner):
    n_ctx, n_fsdp = lax.axis_size("ctx"), lax.axis_size("fsdp")
    pairs = []
    for c in range(n_ctx):
        for f in range(n_fsdp):
            to = partner(c, f)
            if to is not None:
                pairs.append((c * n_fsdp + f, to[0] * n_fsdp + to[1]))
    return lax.ppermute(x, ("ctx", "fsdp"), pairs)


def after(array, done):
    return lax.optimization_barrier((array, done))[0]


def pick(a, i, axis):
    return lax.dynamic_index_in_dim(a, i, axis, keepdims=False)


def reduce_first(x):
    core, low = lax.axis_index("fsdp") % 2, lax.axis_index("fsdp") // 2
    x = pick(x, core, 1) + exchange(pick(x, 1 - core, 1), lambda c, f: (c, f ^ 1))
    own, other = pick(x, low, 0), pick(x, 1 - low, 0)
    beside = exchange(other, lambda c, f: (c, f ^ 2))
    opposite = exchange(own, lambda c, f: (c ^ 4, f))
    across = exchange(other, lambda c, f: (c ^ 4, f ^ 2))
    return own + beside + opposite + across


def reduce_rest(x):
    for partner in (
        lambda c, f: (c ^ 8, f),
        lambda c, f: ((3 - c // 8) * 8 + c % 8, f),
        lambda c, f: (c ^ 1, f),
        lambda c, f: (c // 4 * 4 + 3 - c % 4, f),
    ):
        x = x + exchange(x, partner)
    return x


def per_device(query, gated, grad_out, filters):
    query, gated, grad_out = query[0], gated[0], grad_out[0]
    width = gated.shape[0]
    half = width // 2
    n_ctx = lax.axis_size("ctx")
    me = lax.axis_index("ctx")
    fwd2, left, right, inv_a, inv_b = (jnp.asarray(t) for t in tables())
    up = [(i, (i + 1) % n_ctx) for i in range(n_ctx)]
    down = [(b, a) for a, b in up]

    rows = lambda a, start, size: lax.slice_in_dim(a, start, start + size, axis=0)
    product = lambda o, q, start, size: (rows(o, start, size).astype(F32) * rows(q, start, size).astype(F32)).astype(BF16)
    h_at = lambda start: rows_at(start // GROUP_CH, WIN, BLOCK // GROUP_CH)
    at = lambda start: rows_at(start, FLEN, BLOCK)

    fsdp = lax.axis_index("fsdp")
    far = lax.optimization_barrier(exchange(filters, lambda c, f: (c, f ^ 2)))
    column = jnp.where(fsdp // 2 == 0, jnp.stack([filters, far]), jnp.stack([far, filters])).astype(BF16)
    near = exchange(column, lambda c, f: (c, f ^ 1))
    taps = jnp.where(fsdp % 2 == 0, jnp.stack([column, near], axis=1), jnp.stack([near, column], axis=1)).reshape(-1, FLEN)
    h = dot(jnp.concatenate([taps, taps], axis=1), left)

    sent_a, _ = lax.optimization_barrier((rows(gated, 0, half), far))
    core_b = product(grad_out, query, half, half)
    sent_b, _ = lax.optimization_barrier((core_b, near))
    prev_a = lax.ppermute(sent_a, "ctx", up)
    nxt_b = lax.ppermute(sent_b, "ctx", down)
    late = lax.optimization_barrier((gated, grad_out, query, core_b))[:3]
    core_a = product(late[1], late[2], 0, half)
    prev_b = lax.ppermute(rows(late[0], half, half), "ctx", up)
    nxt_a = lax.ppermute(core_a, "ctx", down)

    full = jax.ShapeDtypeStruct(gated.shape, BF16)
    groups, gblock = width // GROUP_CH, BLOCK // GROUP_CH
    gq, partial = run(
        conv_taps_kernel,
        [(prev_a, at(0)), (gated, at(0)), (grad_out, at(0)), (h, h_at(0)), (core_a, at(0))],
        (fwd2, inv_b, right, inv_a),
        [(full, 0, BLOCK), (jax.ShapeDtypeStruct((groups, FLEN), F32), 0, gblock)],
        half,
    )
    gg, partial = run(
        corr_taps_kernel,
        [(nxt_b, at(0)), (core_b, at(0)), (h, h_at(half)), (gated, at(half))],
        (fwd2, inv_a, left),
        [(full, half, BLOCK), (partial, groups // 2, gblock)],
        half,
    )
    partial = reduce_first(partial.reshape(2, 2, -1, FLEN))
    prev_b, nxt_a, partial = lax.optimization_barrier((prev_b, nxt_a, partial))
    summed = reduce_rest(partial)
    size = half // 2
    for start in (0, size):
        gq, = run(
            conv_kernel,
            [(prev_b, at(start)), (gated, at(half + start)), (grad_out, at(half + start)), (h, h_at(half + start))],
            (fwd2, inv_b),
            [(gq, half + start, BLOCK)],
            size,
            cost=5,
        )
        gg, = run(
            corr_kernel,
            [(nxt_a, at(start)), (core_a, at(start)), (h, h_at(start))],
            (fwd2, inv_a),
            [(gg, start, BLOCK)],
            size,
            cost=5,
        )
    count = lax.axis_size("fsdp") * n_ctx * FLEN * GROUP_CH
    grad_filters = summed * (1.0 / math.sqrt(count))
    return (gq[None], gg[None], grad_filters)


def solution(mesh):
    return jax.shard_map(
        per_device,
        mesh=mesh,
        in_specs=(
            P("fsdp", None, "ctx"),
            P("fsdp", None, "ctx"),
            P("fsdp", None, "ctx"),
            P("fsdp", None),
        ),
        out_specs=(P("fsdp", None, "ctx"), P("fsdp", None, "ctx"), P("fsdp", None)),
        check_vma=False,
    )
```

```python
import math

import jax
import jax.numpy as jnp
import ml_dtypes
import numpy as np
from jax import lax
from jax.experimental import pallas as pl
from jax.experimental.pallas import tpu as pltpu
from jax.sharding import PartitionSpec as P

FLEN = 128
GROUP_CH = 16
WIN = 2 * FLEN
BLOCK = 1024
VMEM_MB = 63
F32, BF16 = jnp.float32, jnp.bfloat16


def split(a):
    hi = a.astype(ml_dtypes.bfloat16)
    lo = (a - hi.astype(np.float64)).astype(ml_dtypes.bfloat16)
    return hi, lo


def tables():
    n = np.arange(WIN)[:, None]
    k = np.arange(FLEN)[None, :]
    angle = np.pi * (((2 * k + 1) * n) % (2 * WIN)) / WIN
    fwd = np.concatenate([np.cos(angle), -np.sin(angle)], axis=1)
    inv = fwd.T / FLEN
    fwd_hi, fwd_lo = split(fwd)
    inv_hi, inv_lo = split(inv)
    fwd2 = np.concatenate([fwd_hi, fwd_lo], axis=0)
    left = np.concatenate([fwd_hi[:FLEN], fwd_lo[:FLEN]], axis=0)
    right = np.concatenate([fwd_hi[FLEN:], fwd_lo[FLEN:]], axis=0)
    pair = lambda cols: np.concatenate([inv_hi[:, cols], inv_lo[:, cols]], axis=1)
    return fwd2, left, right, pair(slice(0, FLEN)), pair(slice(FLEN, WIN))


def dot(a, b):
    return jnp.dot(a, b, preferred_element_type=F32)


def spectrum(first, second, table):
    return dot(jnp.concatenate([first, second, first, second], axis=1), table)


def half_spectrum(block, table):
    return dot(jnp.concatenate([block, block], axis=1), table)


def invert(re, im, table):
    y = dot(jnp.concatenate([re.astype(BF16), im.astype(BF16)], axis=1), table)
    return y[:, :FLEN] + y[:, FLEN:]


def invert_wide(y, table):
    hi = y.astype(BF16)
    lo = (y - hi.astype(F32)).astype(BF16)
    a, b = dot(hi, table), dot(lo, table)
    return a[:, :FLEN] + (a[:, FLEN:] + b[:, :FLEN])


def per_channel(h):
    groups = h.shape[0]
    return jnp.broadcast_to(h[:, None, :], (groups, GROUP_CH, FLEN)).reshape(groups * GROUP_CH, FLEN)


def group_sum(x):
    return jnp.sum(x.reshape(x.shape[0] // GROUP_CH, GROUP_CH, FLEN), axis=1)


def convolve(x, h, table):
    hr, hi = per_channel(h[:, :FLEN]), per_channel(h[:, FLEN:])
    xr, xi = x[:, :FLEN], x[:, FLEN:]
    return invert(xr * hr - xi * hi, xr * hi + xi * hr, table)


def correlate(v, h, table):
    hr, hi = per_channel(h[:, :FLEN]), per_channel(h[:, FLEN:])
    vr, vi = v[:, :FLEN], v[:, FLEN:]
    return invert(vr * hr + vi * hi, vi * hr - vr * hi, table)


def cross(a, b):
    ar, ai, br, bi = a[:, :FLEN], a[:, FLEN:], b[:, :FLEN], b[:, FLEN:]
    return jnp.concatenate([group_sum(ar * br + ai * bi), group_sum(ai * br - ar * bi)], axis=1)


def masked(present, block):
    return jnp.where(present, block, jnp.zeros_like(block))


def has_previous():
    return lax.axis_index("ctx") > 0


def has_next():
    return lax.axis_index("ctx") < lax.axis_size("ctx") - 1


def conv_kernel(prev, cur, gate, h, fwd2, inv_b, gq):
    x = spectrum(masked(has_previous(), prev[...]), cur[...], fwd2[...])
    gq[...] = (gate[...].astype(F32) * convolve(x, h[...], inv_b[...])).astype(BF16)
    return x


def corr_kernel(nxt, core, h, fwd2, inv_a, gg):
    v = spectrum(core[...], masked(has_next(), nxt[...]), fwd2[...])
    gg[...] = correlate(v, h[...], inv_a[...]).astype(BF16)
    return v


def conv_taps_kernel(prev, cur, gate, h, core, fwd2, inv_b, right, inv_a, gq, taps):
    x = conv_kernel(prev, cur, gate, h, fwd2, inv_b, gq)
    taps[...] = invert_wide(cross(half_spectrum(core[...], right[...]), x), inv_a[...])


def corr_taps_kernel(nxt, core, h, cur, fwd2, inv_a, left, gg, taps):
    v = corr_kernel(nxt, core, h, fwd2, inv_a, gg)
    taps[...] = invert_wide(cross(v, half_spectrum(cur[...], left[...])), inv_a[...])


def rows_at(start, width, block):
    return pl.BlockSpec((block, width), lambda i, *_: (start // block + i, 0))


def whole(a):
    return pl.BlockSpec(a.shape, lambda i, *_: (0, 0))


ANY = pl.BlockSpec(memory_space=pl.ANY)


def taps_kernel(column, near, left, h):
    swapped = lax.axis_index("fsdp") % 2 > 0
    table = left[...]
    for low in range(2):
        for core in range(2):
            mine, other = column[low], near[low]
            taps = jnp.where(swapped, other, mine) if core == 0 else jnp.where(swapped, mine, other)
            at = (low * 2 + core) * FLEN
            h[at : at + FLEN, :] = half_spectrum(taps.astype(BF16), table)


def run(kernel, blocks, consts, results, size, cost=0):
    args = [a for a, _ in blocks] + list(consts)
    specs = [s for _, s in blocks] + [whole(c) for c in consts]
    used, aliases = len(args), {}
    for i, (out, _, _) in enumerate(results):
        if not isinstance(out, jax.ShapeDtypeStruct):
            aliases[len(args)] = i
            args.append(out)
            specs.append(ANY)
    given = len(args)

    def body(*refs):
        kernel(*refs[:used], *refs[given:])

    return pl.pallas_call(
        body,
        out_shape=[jax.ShapeDtypeStruct(out.shape, out.dtype) for out, _, _ in results],
        grid=(size // BLOCK,),
        in_specs=specs,
        out_specs=[rows_at(start, FLEN, block) for _, start, block in results],
        input_output_aliases=aliases,
        compiler_params=pltpu.CompilerParams(vmem_limit_bytes=VMEM_MB * 1024 * 1024),
        cost_estimate=pl.CostEstimate(flops=cost * 10**9, bytes_accessed=cost * 10**7, transcendentals=0),
        name=kernel.__name__,
    )(*args)


def exchange(x, partner):
    n_ctx, n_fsdp = lax.axis_size("ctx"), lax.axis_size("fsdp")
    pairs = []
    for c in range(n_ctx):
        for f in range(n_fsdp):
            to = partner(c, f)
            if to is not None:
                pairs.append((c * n_fsdp + f, to[0] * n_fsdp + to[1]))
    return lax.ppermute(x, ("ctx", "fsdp"), pairs)


def after(array, done):
    return lax.optimization_barrier((array, done))[0]


def pick(a, i, axis):
    return lax.dynamic_index_in_dim(a, i, axis, keepdims=False)


def reduce_first(x):
    core, low = lax.axis_index("fsdp") % 2, lax.axis_index("fsdp") // 2
    x = pick(x, core, 1) + exchange(pick(x, 1 - core, 1), lambda c, f: (c, f ^ 1))
    own, other = pick(x, low, 0), pick(x, 1 - low, 0)
    beside = exchange(other, lambda c, f: (c, f ^ 2))
    opposite = exchange(own, lambda c, f: (c ^ 4, f))
    across = exchange(other, lambda c, f: (c ^ 4, f ^ 2))
    return own + beside + opposite + across


def around(x, partners):
    others = [exchange(x, partner) for partner in partners]
    return x + others[0] + others[1] + others[2]


def reduce_rest(x):
    x = around(x, [lambda c, f, step=step: ((c + 8 * step) % 32, f) for step in (1, 3, 2)])
    return around(x, [lambda c, f, step=step: (c // 4 * 4 + (c + step) % 4, f) for step in (1, 3, 2)])


def per_device(query, gated, grad_out, filters):
    query, gated, grad_out = query[0], gated[0], grad_out[0]
    width = gated.shape[0]
    half = width // 2
    n_ctx = lax.axis_size("ctx")
    me = lax.axis_index("ctx")
    fwd2, left, right, inv_a, inv_b = (jnp.asarray(t) for t in tables())
    up = [(i, (i + 1) % n_ctx) for i in range(n_ctx)]
    down = [(b, a) for a, b in up]

    rows = lambda a, start, size: lax.slice_in_dim(a, start, start + size, axis=0)
    product = lambda o, q, start, size: (rows(o, start, size).astype(F32) * rows(q, start, size).astype(F32)).astype(BF16)
    h_at = lambda start: rows_at(start // GROUP_CH, WIN, BLOCK // GROUP_CH)
    at = lambda start: rows_at(start, FLEN, BLOCK)

    fsdp = lax.axis_index("fsdp")
    far = exchange(filters, lambda c, f: (c, f ^ 2))
    column = jnp.where(fsdp // 2 == 0, jnp.stack([filters, far]), jnp.stack([far, filters]))
    near = exchange(column, lambda c, f: (c, f ^ 1))
    h = pl.pallas_call(
        taps_kernel, out_shape=jax.ShapeDtypeStruct((width // GROUP_CH, WIN), F32), name="taps_spectra"
    )(column, near, left)

    sent_a, _ = lax.optimization_barrier((rows(gated, 0, half), far))
    core_b = product(grad_out, query, half, half)
    sent_b, _ = lax.optimization_barrier((core_b, near))
    prev_a = lax.ppermute(sent_a, "ctx", up)
    nxt_b = lax.ppermute(sent_b, "ctx", down)
    late = lax.optimization_barrier((gated, grad_out, query, core_b, near))[:3]
    core_a = product(late[1], late[2], 0, half)
    prev_b = lax.ppermute(rows(late[0], half, half), "ctx", up)
    nxt_a = lax.ppermute(core_a, "ctx", down)

    full = jax.ShapeDtypeStruct(gated.shape, BF16)
    groups, gblock = width // GROUP_CH, BLOCK // GROUP_CH
    gq, partial = run(
        conv_taps_kernel,
        [(prev_a, at(0)), (gated, at(0)), (grad_out, at(0)), (h, h_at(0)), (core_a, at(0))],
        (fwd2, inv_b, right, inv_a),
        [(full, 0, BLOCK), (jax.ShapeDtypeStruct((groups, FLEN), F32), 0, gblock)],
        half,
    )
    gg, partial = run(
        corr_taps_kernel,
        [(nxt_b, at(0)), (core_b, at(0)), (h, h_at(half)), (gated, at(half))],
        (fwd2, inv_a, left),
        [(full, half, BLOCK), (partial, groups // 2, gblock)],
        half,
    )
    partial = reduce_first(partial.reshape(2, 2, -1, FLEN))
    def conv(gq, start, size, cost):
        return run(
            conv_kernel,
            [(prev_b, at(start)), (gated, at(half + start)), (grad_out, at(half + start)), (h, h_at(half + start))],
            (fwd2, inv_b),
            [(gq, half + start, BLOCK)],
            size,
            cost,
        )[0]

    gq = conv(gq, 0, half // 2, 0)
    gq, nxt_a, partial = lax.optimization_barrier((gq, nxt_a, partial))
    summed = reduce_rest(partial)
    gq = conv(gq, half // 2, half // 2, 5)
    gg, = run(
        corr_kernel,
        [(nxt_a, at(0)), (core_a, at(0)), (h, h_at(0))],
        (fwd2, inv_a),
        [(gg, 0, BLOCK)],
        half,
        5,
    )
    count = lax.axis_size("fsdp") * n_ctx * FLEN * GROUP_CH
    grad_filters = summed * (1.0 / math.sqrt(count))
    return (gq[None], gg[None], grad_filters)


def solution(mesh):
    return jax.shard_map(
        per_device,
        mesh=mesh,
        in_specs=(
            P("fsdp", None, "ctx"),
            P("fsdp", None, "ctx"),
            P("fsdp", None, "ctx"),
            P("fsdp", None),
        ),
        out_specs=(P("fsdp", None, "ctx"), P("fsdp", None, "ctx"), P("fsdp", None)),
        check_vma=False,
    )
```

```python
import math

import jax
import jax.numpy as jnp
import ml_dtypes
import numpy as np
from jax import lax
from jax.experimental import pallas as pl
from jax.experimental.pallas import tpu as pltpu
from jax.sharding import PartitionSpec as P

FLEN = 128
GROUP_CH = 16
WIN = 2 * FLEN
BLOCK = 2048
VMEM_MB = 63
F32, BF16 = jnp.float32, jnp.bfloat16


def split(a):
    hi = a.astype(ml_dtypes.bfloat16)
    lo = (a - hi.astype(np.float64)).astype(ml_dtypes.bfloat16)
    return hi, lo


def tables():
    n = np.arange(WIN)[:, None]
    k = np.arange(FLEN)[None, :]
    angle = np.pi * (((2 * k + 1) * n) % (2 * WIN)) / WIN
    fwd = np.concatenate([np.cos(angle), -np.sin(angle)], axis=1)
    inv = fwd.T / FLEN
    fwd_hi, fwd_lo = split(fwd)
    inv_hi, inv_lo = split(inv)
    fwd2 = np.concatenate([fwd_hi, fwd_lo], axis=0)
    left = np.concatenate([fwd_hi[:FLEN], fwd_lo[:FLEN]], axis=0)
    right = np.concatenate([fwd_hi[FLEN:], fwd_lo[FLEN:]], axis=0)
    pair = lambda cols: np.concatenate([inv_hi[:, cols], inv_lo[:, cols]], axis=1)
    return fwd2, left, right, pair(slice(0, FLEN)), pair(slice(FLEN, WIN))


def dot(a, b):
    return jnp.dot(a, b, preferred_element_type=F32)


def spectrum(first, second, table):
    return dot(jnp.concatenate([first, second, first, second], axis=1), table)


def half_spectrum(block, table):
    return dot(jnp.concatenate([block, block], axis=1), table)


def invert(re, im, table):
    y = dot(jnp.concatenate([re.astype(BF16), im.astype(BF16)], axis=1), table)
    return y[:, :FLEN] + y[:, FLEN:]


def invert_wide(y, table):
    hi = y.astype(BF16)
    lo = (y - hi.astype(F32)).astype(BF16)
    a, b = dot(hi, table), dot(lo, table)
    return a[:, :FLEN] + (a[:, FLEN:] + b[:, :FLEN])


def per_channel(h):
    groups = h.shape[0]
    return jnp.broadcast_to(h[:, None, :], (groups, GROUP_CH, FLEN)).reshape(groups * GROUP_CH, FLEN)


def group_sum(x):
    return jnp.sum(x.reshape(x.shape[0] // GROUP_CH, GROUP_CH, FLEN), axis=1)


def convolve(x, h, table):
    hr, hi = per_channel(h[:, :FLEN]), per_channel(h[:, FLEN:])
    xr, xi = x[:, :FLEN], x[:, FLEN:]
    return invert(xr * hr - xi * hi, xr * hi + xi * hr, table)


def correlate(v, h, table):
    hr, hi = per_channel(h[:, :FLEN]), per_channel(h[:, FLEN:])
    vr, vi = v[:, :FLEN], v[:, FLEN:]
    return invert(vr * hr + vi * hi, vi * hr - vr * hi, table)


def cross(a, b):
    ar, ai, br, bi = a[:, :FLEN], a[:, FLEN:], b[:, :FLEN], b[:, FLEN:]
    return jnp.concatenate([group_sum(ar * br + ai * bi), group_sum(ai * br - ar * bi)], axis=1)


def masked(present, block):
    return jnp.where(present, block, jnp.zeros_like(block))


def has_previous():
    return lax.axis_index("ctx") > 0


def has_next():
    return lax.axis_index("ctx") < lax.axis_size("ctx") - 1


def conv_kernel(prev, cur, gate, h, fwd2, inv_b, gq):
    x = spectrum(masked(has_previous(), prev[...]), cur[...], fwd2[...])
    gq[...] = (gate[...].astype(F32) * convolve(x, h[...], inv_b[...])).astype(BF16)
    return x


def corr_kernel(nxt, core, h, fwd2, inv_a, gg):
    v = spectrum(core[...], masked(has_next(), nxt[...]), fwd2[...])
    gg[...] = correlate(v, h[...], inv_a[...]).astype(BF16)
    return v


def conv_taps_kernel(prev, cur, gate, h, core, fwd2, inv_b, right, inv_a, gq, taps):
    x = conv_kernel(prev, cur, gate, h, fwd2, inv_b, gq)
    taps[...] = invert_wide(cross(half_spectrum(core[...], right[...]), x), inv_a[...])


def corr_taps_kernel(nxt, core, h, cur, fwd2, inv_a, left, gg, taps):
    v = corr_kernel(nxt, core, h, fwd2, inv_a, gg)
    taps[...] = invert_wide(cross(v, half_spectrum(cur[...], left[...])), inv_a[...])


def rows_at(start, width, block):
    return pl.BlockSpec((block, width), lambda i, *_: (start // block + i, 0))


def whole(a):
    return pl.BlockSpec(a.shape, lambda i, *_: (0, 0))


ANY = pl.BlockSpec(memory_space=pl.ANY)


def taps_kernel(column, near, left, h):
    swapped = lax.axis_index("fsdp") % 2 > 0
    table = left[...]
    for low in range(2):
        for core in range(2):
            mine, other = column[low], near[low]
            taps = jnp.where(swapped, other, mine) if core == 0 else jnp.where(swapped, mine, other)
            at = (low * 2 + core) * FLEN
            h[at : at + FLEN, :] = half_spectrum(taps.astype(BF16), table)


def run(kernel, blocks, consts, results, size, cost=0):
    args = [a for a, _ in blocks] + list(consts)
    specs = [s for _, s in blocks] + [whole(c) for c in consts]
    used, aliases = len(args), {}
    for i, (out, _, _) in enumerate(results):
        if not isinstance(out, jax.ShapeDtypeStruct):
            aliases[len(args)] = i
            args.append(out)
            specs.append(ANY)
    given = len(args)

    def body(*refs):
        kernel(*refs[:used], *refs[given:])

    return pl.pallas_call(
        body,
        out_shape=[jax.ShapeDtypeStruct(out.shape, out.dtype) for out, _, _ in results],
        grid=(size // BLOCK,),
        in_specs=specs,
        out_specs=[rows_at(start, FLEN, block) for _, start, block in results],
        input_output_aliases=aliases,
        compiler_params=pltpu.CompilerParams(vmem_limit_bytes=VMEM_MB * 1024 * 1024),
        cost_estimate=pl.CostEstimate(flops=cost * 10**9, bytes_accessed=cost * 10**7, transcendentals=0),
        name=kernel.__name__,
    )(*args)


def exchange(x, partner):
    n_ctx, n_fsdp = lax.axis_size("ctx"), lax.axis_size("fsdp")
    pairs = []
    for c in range(n_ctx):
        for f in range(n_fsdp):
            to = partner(c, f)
            if to is not None:
                pairs.append((c * n_fsdp + f, to[0] * n_fsdp + to[1]))
    return lax.ppermute(x, ("ctx", "fsdp"), pairs)


def after(array, done):
    return lax.optimization_barrier((array, done))[0]


def pick(a, i, axis):
    return lax.dynamic_index_in_dim(a, i, axis, keepdims=False)


def reduce_first(x):
    core, low = lax.axis_index("fsdp") % 2, lax.axis_index("fsdp") // 2
    x = pick(x, core, 1) + exchange(pick(x, 1 - core, 1), lambda c, f: (c, f ^ 1))
    own, other = pick(x, low, 0), pick(x, 1 - low, 0)
    beside = exchange(other, lambda c, f: (c, f ^ 2))
    opposite = exchange(own, lambda c, f: (c ^ 4, f))
    across = exchange(other, lambda c, f: (c ^ 4, f ^ 2))
    return own + beside + opposite + across


def around(x, partners):
    others = [exchange(x, partner) for partner in partners]
    return x + others[0] + others[1] + others[2]


def reduce_rest(x):
    x = around(x, [lambda c, f, step=step: ((c + 8 * step) % 32, f) for step in (1, 3, 2)])
    return around(x, [lambda c, f, step=step: (c // 4 * 4 + (c + step) % 4, f) for step in (1, 3, 2)])


def per_device(query, gated, grad_out, filters):
    query, gated, grad_out = query[0], gated[0], grad_out[0]
    width = gated.shape[0]
    half = width // 2
    n_ctx = lax.axis_size("ctx")
    me = lax.axis_index("ctx")
    fwd2, left, right, inv_a, inv_b = (jnp.asarray(t) for t in tables())
    up = [(i, (i + 1) % n_ctx) for i in range(n_ctx)]
    down = [(b, a) for a, b in up]

    rows = lambda a, start, size: lax.slice_in_dim(a, start, start + size, axis=0)
    product = lambda o, q, start, size: (rows(o, start, size).astype(F32) * rows(q, start, size).astype(F32)).astype(BF16)
    h_at = lambda start: rows_at(start // GROUP_CH, WIN, BLOCK // GROUP_CH)
    at = lambda start: rows_at(start, FLEN, BLOCK)

    fsdp = lax.axis_index("fsdp")
    far = exchange(filters, lambda c, f: (c, f ^ 2))
    column = jnp.where(fsdp // 2 == 0, jnp.stack([filters, far]), jnp.stack([far, filters]))
    core_b = product(grad_out, query, half, half)
    sent_b, column = lax.optimization_barrier((core_b, column))
    near = exchange(column, lambda c, f: (c, f ^ 1))
    h = pl.pallas_call(
        taps_kernel, out_shape=jax.ShapeDtypeStruct((width // GROUP_CH, WIN), F32), name="taps_spectra"
    )(column, near, left)

    sent_a, _ = lax.optimization_barrier((rows(gated, 0, half), far))
    prev_a = lax.ppermute(sent_a, "ctx", up)
    nxt_b = lax.ppermute(sent_b, "ctx", down)
    late = lax.optimization_barrier((gated, grad_out, query, core_b, near))[:3]
    core_a = product(late[1], late[2], 0, half)
    prev_b = lax.ppermute(rows(late[0], half, half), "ctx", up)
    nxt_a = lax.ppermute(core_a, "ctx", down)

    full = jax.ShapeDtypeStruct(gated.shape, BF16)
    groups, gblock = width // GROUP_CH, BLOCK // GROUP_CH
    gq, partial = run(
        conv_taps_kernel,
        [(prev_a, at(0)), (gated, at(0)), (grad_out, at(0)), (h, h_at(0)), (core_a, at(0))],
        (fwd2, inv_b, right, inv_a),
        [(full, 0, BLOCK), (jax.ShapeDtypeStruct((groups, FLEN), F32), 0, gblock)],
        half,
    )
    gg, partial = run(
        corr_taps_kernel,
        [(nxt_b, at(0)), (core_b, at(0)), (h, h_at(half)), (gated, at(half))],
        (fwd2, inv_a, left),
        [(full, half, BLOCK), (partial, groups // 2, gblock)],
        half,
    )
    partial = reduce_first(partial.reshape(2, 2, -1, FLEN))
    prev_b, nxt_a, partial = lax.optimization_barrier((prev_b, nxt_a, partial))
    summed = reduce_rest(partial)
    gq, = run(
        conv_kernel,
        [(prev_b, at(0)), (gated, at(half)), (grad_out, at(half)), (h, h_at(half))],
        (fwd2, inv_b),
        [(gq, half, BLOCK)],
        half,
        5,
    )
    gg, = run(
        corr_kernel,
        [(nxt_a, at(0)), (core_a, at(0)), (h, h_at(0))],
        (fwd2, inv_a),
        [(gg, 0, BLOCK)],
        half,
        5,
    )
    count = lax.axis_size("fsdp") * n_ctx * FLEN * GROUP_CH
    grad_filters = summed * (1.0 / math.sqrt(count))
    return (gq[None], gg[None], grad_filters)


def solution(mesh):
    return jax.shard_map(
        per_device,
        mesh=mesh,
        in_specs=(
            P("fsdp", None, "ctx"),
            P("fsdp", None, "ctx"),
            P("fsdp", None, "ctx"),
            P("fsdp", None),
        ),
        out_specs=(P("fsdp", None, "ctx"), P("fsdp", None, "ctx"), P("fsdp", None)),
        check_vma=False,
    )
```

```python
import math

import jax
import jax.numpy as jnp
import ml_dtypes
import numpy as np
from jax import lax
from jax.experimental import pallas as pl
from jax.experimental.pallas import tpu as pltpu
from jax.sharding import PartitionSpec as P

FLEN = 128
GROUP_CH = 16
WIN = 2 * FLEN
BLOCK = 2048
VMEM_MB = 63
F32, BF16 = jnp.float32, jnp.bfloat16


def split(a):
    hi = a.astype(ml_dtypes.bfloat16)
    lo = (a - hi.astype(np.float64)).astype(ml_dtypes.bfloat16)
    return hi, lo


def tables():
    n = np.arange(WIN)[:, None]
    k = np.arange(FLEN)[None, :]
    angle = np.pi * (((2 * k + 1) * n) % (2 * WIN)) / WIN
    fwd = np.concatenate([np.cos(angle), -np.sin(angle)], axis=1)
    inv = fwd.T / FLEN
    fwd_hi, fwd_lo = split(fwd)
    inv_hi, inv_lo = split(inv)
    fwd2 = np.concatenate([fwd_hi, fwd_lo], axis=0)
    left = np.concatenate([fwd_hi[:FLEN], fwd_lo[:FLEN]], axis=0)
    right = np.concatenate([fwd_hi[FLEN:], fwd_lo[FLEN:]], axis=0)
    pair = lambda cols: np.concatenate([inv_hi[:, cols], inv_lo[:, cols]], axis=1)
    return fwd2, left, right, pair(slice(0, FLEN)), pair(slice(FLEN, WIN))


def dot(a, b):
    return jnp.dot(a, b, preferred_element_type=F32)


def spectrum(first, second, table):
    return dot(jnp.concatenate([first, second, first, second], axis=1), table)


def half_spectrum(block, table):
    return dot(jnp.concatenate([block, block], axis=1), table)


def invert(re, im, table):
    y = dot(jnp.concatenate([re.astype(BF16), im.astype(BF16)], axis=1), table)
    return y[:, :FLEN] + y[:, FLEN:]


def invert_wide(y, table):
    hi = y.astype(BF16)
    lo = (y - hi.astype(F32)).astype(BF16)
    a, b = dot(hi, table), dot(lo, table)
    return a[:, :FLEN] + (a[:, FLEN:] + b[:, :FLEN])


def per_channel(h):
    groups = h.shape[0]
    return jnp.broadcast_to(h[:, None, :], (groups, GROUP_CH, FLEN)).reshape(groups * GROUP_CH, FLEN)


def group_sum(x):
    return jnp.sum(x.reshape(x.shape[0] // GROUP_CH, GROUP_CH, FLEN), axis=1)


def convolve(x, h, table):
    hr, hi = per_channel(h[:, :FLEN]), per_channel(h[:, FLEN:])
    xr, xi = x[:, :FLEN], x[:, FLEN:]
    return invert(xr * hr - xi * hi, xr * hi + xi * hr, table)


def correlate(v, h, table):
    hr, hi = per_channel(h[:, :FLEN]), per_channel(h[:, FLEN:])
    vr, vi = v[:, :FLEN], v[:, FLEN:]
    return invert(vr * hr + vi * hi, vi * hr - vr * hi, table)


def cross(a, b):
    ar, ai, br, bi = a[:, :FLEN], a[:, FLEN:], b[:, :FLEN], b[:, FLEN:]
    return jnp.concatenate([group_sum(ar * br + ai * bi), group_sum(ai * br - ar * bi)], axis=1)


def masked(present, block):
    return jnp.where(present, block, jnp.zeros_like(block))


def has_previous():
    return lax.axis_index("ctx") > 0


def has_next():
    return lax.axis_index("ctx") < lax.axis_size("ctx") - 1


def conv_kernel(prev, cur, gate, h, fwd2, inv_b, gq):
    x = spectrum(masked(has_previous(), prev[...]), cur[...], fwd2[...])
    gq[...] = (gate[...].astype(F32) * convolve(x, h[...], inv_b[...])).astype(BF16)
    return x


def corr_kernel(nxt, core, h, fwd2, inv_a, gg):
    v = spectrum(core[...], masked(has_next(), nxt[...]), fwd2[...])
    gg[...] = correlate(v, h[...], inv_a[...]).astype(BF16)
    return v


def conv_taps_kernel(prev, cur, gate, h, core, fwd2, inv_b, right, inv_a, gq, taps):
    x = conv_kernel(prev, cur, gate, h, fwd2, inv_b, gq)
    taps[...] = invert_wide(cross(half_spectrum(core[...], right[...]), x), inv_a[...])


def corr_taps_kernel(nxt, core, h, cur, fwd2, inv_a, left, gg, taps):
    v = corr_kernel(nxt, core, h, fwd2, inv_a, gg)
    taps[...] = invert_wide(cross(v, half_spectrum(cur[...], left[...])), inv_a[...])


def rows_at(start, width, block):
    return pl.BlockSpec((block, width), lambda i, *_: (start // block + i, 0))


def whole(a):
    return pl.BlockSpec(a.shape, lambda i, *_: (0, 0))


ANY = pl.BlockSpec(memory_space=pl.ANY)


def taps_kernel(column, near, left, h):
    swapped = lax.axis_index("fsdp") % 2 > 0
    table = left[...]
    for low in range(2):
        for core in range(2):
            mine, other = column[low], near[low]
            taps = jnp.where(swapped, other, mine) if core == 0 else jnp.where(swapped, mine, other)
            at = (low * 2 + core) * FLEN
            h[at : at + FLEN, :] = half_spectrum(taps.astype(BF16), table)


def run(kernel, blocks, consts, results, size, cost=0):
    args = [a for a, _ in blocks] + list(consts)
    specs = [s for _, s in blocks] + [whole(c) for c in consts]
    used, aliases = len(args), {}
    for i, (out, _, _) in enumerate(results):
        if not isinstance(out, jax.ShapeDtypeStruct):
            aliases[len(args)] = i
            args.append(out)
            specs.append(ANY)
    given = len(args)

    def body(*refs):
        kernel(*refs[:used], *refs[given:])

    return pl.pallas_call(
        body,
        out_shape=[jax.ShapeDtypeStruct(out.shape, out.dtype) for out, _, _ in results],
        grid=(size // BLOCK,),
        in_specs=specs,
        out_specs=[rows_at(start, FLEN, block) for _, start, block in results],
        input_output_aliases=aliases,
        compiler_params=pltpu.CompilerParams(vmem_limit_bytes=VMEM_MB * 1024 * 1024),
        cost_estimate=pl.CostEstimate(flops=cost * 10**9, bytes_accessed=cost * 10**7, transcendentals=0),
        name=kernel.__name__,
    )(*args)


def exchange(x, partner):
    n_ctx, n_fsdp = lax.axis_size("ctx"), lax.axis_size("fsdp")
    pairs = []
    for c in range(n_ctx):
        for f in range(n_fsdp):
            to = partner(c, f)
            if to is not None:
                pairs.append((c * n_fsdp + f, to[0] * n_fsdp + to[1]))
    return lax.ppermute(x, ("ctx", "fsdp"), pairs)


def after(array, done):
    return lax.optimization_barrier((array, done))[0]


def pick(a, i, axis):
    return lax.dynamic_index_in_dim(a, i, axis, keepdims=False)


def reduce_first(x):
    core, low = lax.axis_index("fsdp") % 2, lax.axis_index("fsdp") // 2
    x = pick(x, core, 1) + exchange(pick(x, 1 - core, 1), lambda c, f: (c, f ^ 1))
    own, other = pick(x, low, 0), pick(x, 1 - low, 0)
    beside = exchange(other, lambda c, f: (c, f ^ 2))
    opposite = exchange(own, lambda c, f: (c ^ 4, f))
    across = exchange(other, lambda c, f: (c ^ 4, f ^ 2))
    return own + beside + opposite + across


def around(x, partners):
    others = [exchange(x, partner) for partner in partners]
    return x + others[0] + others[1] + others[2]


def reduce_rest(x):
    x = around(x, [lambda c, f, step=step: (c // 4 * 4 + (c + step) % 4, f) for step in (1, 3, 2)])
    return around(x, [lambda c, f, step=step: ((c + 8 * step) % 32, f) for step in (1, 3, 2)])


def per_device(query, gated, grad_out, filters):
    query, gated, grad_out = query[0], gated[0], grad_out[0]
    width = gated.shape[0]
    half = width // 2
    n_ctx = lax.axis_size("ctx")
    me = lax.axis_index("ctx")
    fwd2, left, right, inv_a, inv_b = (jnp.asarray(t) for t in tables())
    up = [(i, (i + 1) % n_ctx) for i in range(n_ctx)]
    down = [(b, a) for a, b in up]

    rows = lambda a, start, size: lax.slice_in_dim(a, start, start + size, axis=0)
    product = lambda o, q, start, size: (rows(o, start, size).astype(F32) * rows(q, start, size).astype(F32)).astype(BF16)
    h_at = lambda start: rows_at(start // GROUP_CH, WIN, BLOCK // GROUP_CH)
    at = lambda start: rows_at(start, FLEN, BLOCK)

    fsdp = lax.axis_index("fsdp")
    far = exchange(filters, lambda c, f: (c, f ^ 2))
    column = jnp.where(fsdp // 2 == 0, jnp.stack([filters, far]), jnp.stack([far, filters]))
    core_b = product(grad_out, query, half, half)
    sent_b, column = lax.optimization_barrier((core_b, column))
    near = exchange(column, lambda c, f: (c, f ^ 1))
    h = pl.pallas_call(
        taps_kernel, out_shape=jax.ShapeDtypeStruct((width // GROUP_CH, WIN), F32), name="taps_spectra"
    )(column, near, left)

    sent_a, _ = lax.optimization_barrier((rows(gated, 0, half), far))
    prev_a = lax.ppermute(sent_a, "ctx", up)
    nxt_b = lax.ppermute(sent_b, "ctx", down)
    late = lax.optimization_barrier((gated, grad_out, query, core_b, near))[:3]
    core_a = product(late[1], late[2], 0, half)
    prev_b = lax.ppermute(rows(late[0], half, half), "ctx", up)
    nxt_a = lax.ppermute(core_a, "ctx", down)

    full = jax.ShapeDtypeStruct(gated.shape, BF16)
    groups, gblock = width // GROUP_CH, BLOCK // GROUP_CH
    gq, partial = run(
        conv_taps_kernel,
        [(prev_a, at(0)), (gated, at(0)), (grad_out, at(0)), (h, h_at(0)), (core_a, at(0))],
        (fwd2, inv_b, right, inv_a),
        [(full, 0, BLOCK), (jax.ShapeDtypeStruct((groups, FLEN), F32), 0, gblock)],
        half,
    )
    gg, partial = run(
        corr_taps_kernel,
        [(nxt_b, at(0)), (core_b, at(0)), (h, h_at(half)), (gated, at(half))],
        (fwd2, inv_a, left),
        [(full, half, BLOCK), (partial, groups // 2, gblock)],
        half,
    )
    partial = reduce_first(partial.reshape(2, 2, -1, FLEN))
    prev_b, nxt_a, partial = lax.optimization_barrier((prev_b, nxt_a, partial))
    summed = reduce_rest(partial)
    gq, = run(
        conv_kernel,
        [(prev_b, at(0)), (gated, at(half)), (grad_out, at(half)), (h, h_at(half))],
        (fwd2, inv_b),
        [(gq, half, BLOCK)],
        half,
        5,
    )
    gg, = run(
        corr_kernel,
        [(nxt_a, at(0)), (core_a, at(0)), (h, h_at(0))],
        (fwd2, inv_a),
        [(gg, 0, BLOCK)],
        half,
        5,
    )
    count = lax.axis_size("fsdp") * n_ctx * FLEN * GROUP_CH
    grad_filters = summed * (1.0 / math.sqrt(count))
    return (gq[None], gg[None], grad_filters)


def solution(mesh):
    return jax.shard_map(
        per_device,
        mesh=mesh,
        in_specs=(
            P("fsdp", None, "ctx"),
            P("fsdp", None, "ctx"),
            P("fsdp", None, "ctx"),
            P("fsdp", None),
        ),
        out_specs=(P("fsdp", None, "ctx"), P("fsdp", None, "ctx"), P("fsdp", None)),
        check_vma=False,
    )
```

```python
import math

import jax
import jax.numpy as jnp
import ml_dtypes
import numpy as np
from jax import lax
from jax.experimental import pallas as pl
from jax.experimental.pallas import tpu as pltpu
from jax.sharding import PartitionSpec as P

FLEN = 128
GROUP_CH = 16
WIN = 2 * FLEN
BLOCK = 2048
VMEM_MB = 63
F32, BF16 = jnp.float32, jnp.bfloat16


def split(a):
    hi = a.astype(ml_dtypes.bfloat16)
    lo = (a - hi.astype(np.float64)).astype(ml_dtypes.bfloat16)
    return hi, lo


def tables():
    n = np.arange(WIN)[:, None]
    k = np.arange(FLEN)[None, :]
    angle = np.pi * (((2 * k + 1) * n) % (2 * WIN)) / WIN
    fwd = np.concatenate([np.cos(angle), -np.sin(angle)], axis=1)
    inv = fwd.T / FLEN
    fwd_hi, fwd_lo = split(fwd)
    inv_hi, inv_lo = split(inv)
    fwd2 = np.concatenate([fwd_hi, fwd_lo], axis=0)
    left = np.concatenate([fwd_hi[:FLEN], fwd_lo[:FLEN]], axis=0)
    right = np.concatenate([fwd_hi[FLEN:], fwd_lo[FLEN:]], axis=0)
    pair = lambda cols: np.concatenate([inv_hi[:, cols], inv_lo[:, cols]], axis=1)
    return fwd2, left, right, pair(slice(0, FLEN)), pair(slice(FLEN, WIN))


def dot(a, b):
    return jnp.dot(a, b, preferred_element_type=F32)


def spectrum(first, second, table):
    return dot(jnp.concatenate([first, second, first, second], axis=1), table)


def half_spectrum(block, table):
    return dot(jnp.concatenate([block, block], axis=1), table)


def invert(re, im, table):
    y = dot(jnp.concatenate([re.astype(BF16), im.astype(BF16)], axis=1), table)
    return y[:, :FLEN] + y[:, FLEN:]


def invert_wide(y, table):
    hi = y.astype(BF16)
    lo = (y - hi.astype(F32)).astype(BF16)
    a, b = dot(hi, table), dot(lo, table)
    return a[:, :FLEN] + (a[:, FLEN:] + b[:, :FLEN])


def per_channel(h):
    groups = h.shape[0]
    return jnp.broadcast_to(h[:, None, :], (groups, GROUP_CH, FLEN)).reshape(groups * GROUP_CH, FLEN)


def group_sum(x):
    return jnp.sum(x.reshape(x.shape[0] // GROUP_CH, GROUP_CH, FLEN), axis=1)


def convolve(x, h, table):
    hr, hi = per_channel(h[:, :FLEN]), per_channel(h[:, FLEN:])
    xr, xi = x[:, :FLEN], x[:, FLEN:]
    return invert(xr * hr - xi * hi, xr * hi + xi * hr, table)


def correlate(v, h, table):
    hr, hi = per_channel(h[:, :FLEN]), per_channel(h[:, FLEN:])
    vr, vi = v[:, :FLEN], v[:, FLEN:]
    return invert(vr * hr + vi * hi, vi * hr - vr * hi, table)


def cross(a, b):
    ar, ai, br, bi = a[:, :FLEN], a[:, FLEN:], b[:, :FLEN], b[:, FLEN:]
    return jnp.concatenate([group_sum(ar * br + ai * bi), group_sum(ai * br - ar * bi)], axis=1)


def masked(present, block):
    return jnp.where(present, block, jnp.zeros_like(block))


def has_previous():
    return lax.axis_index("ctx") > 0


def has_next():
    return lax.axis_index("ctx") < lax.axis_size("ctx") - 1


def conv_kernel(prev, cur, gate, h, fwd2, inv_b, gq):
    x = spectrum(masked(has_previous(), prev[...]), cur[...], fwd2[...])
    gq[...] = (gate[...].astype(F32) * convolve(x, h[...], inv_b[...])).astype(BF16)
    return x


def corr_kernel(nxt, core, h, fwd2, inv_a, gg):
    v = spectrum(core[...], masked(has_next(), nxt[...]), fwd2[...])
    gg[...] = correlate(v, h[...], inv_a[...]).astype(BF16)
    return v


def conv_taps_kernel(prev, cur, gate, h, core, fwd2, inv_b, right, inv_a, gq, taps):
    x = conv_kernel(prev, cur, gate, h, fwd2, inv_b, gq)
    taps[...] = invert_wide(cross(half_spectrum(core[...], right[...]), x), inv_a[...])


def corr_taps_kernel(nxt, core, h, cur, fwd2, inv_a, left, gg, taps):
    v = corr_kernel(nxt, core, h, fwd2, inv_a, gg)
    taps[...] = invert_wide(cross(v, half_spectrum(cur[...], left[...])), inv_a[...])


def rows_at(start, width, block):
    return pl.BlockSpec((block, width), lambda i, *_: (start // block + i, 0))


def whole(a):
    return pl.BlockSpec(a.shape, lambda i, *_: (0, 0))


ANY = pl.BlockSpec(memory_space=pl.ANY)


def taps_kernel(column, near, left, h):
    swapped = lax.axis_index("fsdp") % 2 > 0
    table = left[...]
    for low in range(2):
        for core in range(2):
            mine, other = column[low], near[low]
            taps = jnp.where(swapped, other, mine) if core == 0 else jnp.where(swapped, mine, other)
            at = (low * 2 + core) * FLEN
            h[at : at + FLEN, :] = half_spectrum(taps.astype(BF16), table)


def run(kernel, blocks, consts, results, size, cost=0, block=BLOCK):
    args = [a for a, _ in blocks] + list(consts)
    specs = [s for _, s in blocks] + [whole(c) for c in consts]
    used, aliases = len(args), {}
    for i, (out, _, _) in enumerate(results):
        if not isinstance(out, jax.ShapeDtypeStruct):
            aliases[len(args)] = i
            args.append(out)
            specs.append(ANY)
    given = len(args)

    def body(*refs):
        kernel(*refs[:used], *refs[given:])

    return pl.pallas_call(
        body,
        out_shape=[jax.ShapeDtypeStruct(out.shape, out.dtype) for out, _, _ in results],
        grid=(size // block,),
        in_specs=specs,
        out_specs=[rows_at(start, FLEN, n) for _, start, n in results],
        input_output_aliases=aliases,
        compiler_params=pltpu.CompilerParams(vmem_limit_bytes=VMEM_MB * 1024 * 1024),
        cost_estimate=pl.CostEstimate(flops=cost * 10**9, bytes_accessed=cost * 10**7, transcendentals=0),
        name=kernel.__name__,
    )(*args)


def exchange(x, partner):
    n_ctx, n_fsdp = lax.axis_size("ctx"), lax.axis_size("fsdp")
    pairs = []
    for c in range(n_ctx):
        for f in range(n_fsdp):
            to = partner(c, f)
            if to is not None:
                pairs.append((c * n_fsdp + f, to[0] * n_fsdp + to[1]))
    return lax.ppermute(x, ("ctx", "fsdp"), pairs)


def after(array, done):
    return lax.optimization_barrier((array, done))[0]


def pick(a, i, axis):
    return lax.dynamic_index_in_dim(a, i, axis, keepdims=False)


def reduce_first(x):
    core, low = lax.axis_index("fsdp") % 2, lax.axis_index("fsdp") // 2
    x = pick(x, core, 1) + exchange(pick(x, 1 - core, 1), lambda c, f: (c, f ^ 1))
    own, other = pick(x, low, 0), pick(x, 1 - low, 0)
    beside = exchange(other, lambda c, f: (c, f ^ 2))
    opposite = exchange(own, lambda c, f: (c ^ 4, f))
    across = exchange(other, lambda c, f: (c ^ 4, f ^ 2))
    return own + beside + opposite + across


def around(x, partners):
    others = [exchange(x, partner) for partner in partners]
    return x + others[0] + others[1] + others[2]


def reduce_rest(x):
    x = around(x, [lambda c, f, step=step: ((c + 8 * step) % 32, f) for step in (1, 3, 2)])
    return around(x, [lambda c, f, step=step: (c // 4 * 4 + (c + step) % 4, f) for step in (1, 3, 2)])


def per_device(query, gated, grad_out, filters):
    query, gated, grad_out = query[0], gated[0], grad_out[0]
    width = gated.shape[0]
    half = width // 2
    n_ctx = lax.axis_size("ctx")
    me = lax.axis_index("ctx")
    fwd2, left, right, inv_a, inv_b = (jnp.asarray(t) for t in tables())
    up = [(i, (i + 1) % n_ctx) for i in range(n_ctx)]
    down = [(b, a) for a, b in up]

    rows = lambda a, start, size: lax.slice_in_dim(a, start, start + size, axis=0)
    product = lambda o, q, start, size: (rows(o, start, size).astype(F32) * rows(q, start, size).astype(F32)).astype(BF16)
    h_at = lambda start: rows_at(start // GROUP_CH, WIN, BLOCK // GROUP_CH)
    at = lambda start: rows_at(start, FLEN, BLOCK)

    fsdp = lax.axis_index("fsdp")
    far = exchange(filters, lambda c, f: (c, f ^ 2))
    column = jnp.where(fsdp // 2 == 0, jnp.stack([filters, far]), jnp.stack([far, filters]))
    core_b = product(grad_out, query, half, half)
    sent_b, column = lax.optimization_barrier((core_b, column))
    near = exchange(column, lambda c, f: (c, f ^ 1))
    h = pl.pallas_call(
        taps_kernel, out_shape=jax.ShapeDtypeStruct((width // GROUP_CH, WIN), F32), name="taps_spectra"
    )(column, near, left)

    sent_a, _ = lax.optimization_barrier((rows(gated, 0, half), far))
    prev_a = lax.ppermute(sent_a, "ctx", up)
    nxt_b = lax.ppermute(sent_b, "ctx", down)
    late = lax.optimization_barrier((gated, grad_out, query, core_b, near))[:3]
    core_a = product(late[1], late[2], 0, half)
    prev_b = lax.ppermute(rows(late[0], half, half), "ctx", up)
    nxt_a = lax.ppermute(core_a, "ctx", down)

    full = jax.ShapeDtypeStruct(gated.shape, BF16)
    groups, gblock = width // GROUP_CH, BLOCK // GROUP_CH
    gq, partial = run(
        conv_taps_kernel,
        [(prev_a, at(0)), (gated, at(0)), (grad_out, at(0)), (h, h_at(0)), (core_a, at(0))],
        (fwd2, inv_b, right, inv_a),
        [(full, 0, BLOCK), (jax.ShapeDtypeStruct((groups, FLEN), F32), 0, gblock)],
        half,
    )
    gg, partial = run(
        corr_taps_kernel,
        [(nxt_b, at(0)), (core_b, at(0)), (h, h_at(half)), (gated, at(half))],
        (fwd2, inv_a, left),
        [(full, half, BLOCK), (partial, groups // 2, gblock)],
        half,
    )
    partial = reduce_first(partial.reshape(2, 2, -1, FLEN))
    def conv(gq, start, size, cost):
        n = 1024
        part = lambda first: rows_at(first, FLEN, n)
        return run(
            conv_kernel,
            [(prev_b, part(start)), (gated, part(half + start)), (grad_out, part(half + start)),
             (h, rows_at((half + start) // GROUP_CH, WIN, n // GROUP_CH))],
            (fwd2, inv_b),
            [(gq, half + start, n)],
            size,
            cost,
            n,
        )[0]

    gq = conv(gq, 0, 1024, 0)
    gq, nxt_a, partial = lax.optimization_barrier((gq, nxt_a, partial))
    summed = reduce_rest(partial)
    gq = conv(gq, 1024, half - 1024, 5)
    gg, = run(
        corr_kernel,
        [(nxt_a, at(0)), (core_a, at(0)), (h, h_at(0))],
        (fwd2, inv_a),
        [(gg, 0, BLOCK)],
        half,
        5,
    )
    count = lax.axis_size("fsdp") * n_ctx * FLEN * GROUP_CH
    grad_filters = summed * (1.0 / math.sqrt(count))
    return (gq[None], gg[None], grad_filters)


def solution(mesh):
    return jax.shard_map(
        per_device,
        mesh=mesh,
        in_specs=(
            P("fsdp", None, "ctx"),
            P("fsdp", None, "ctx"),
            P("fsdp", None, "ctx"),
            P("fsdp", None),
        ),
        out_specs=(P("fsdp", None, "ctx"), P("fsdp", None, "ctx"), P("fsdp", None)),
        check_vma=False,
    )
```
